32 devices in a mesh: grp: 2 (over y), ja: 4 (over z), ia: 4 (over x, core).
Axes of the slice: x: 2, y: 2, z: 4, core: 2. Of those that a mesh axis runs over, the one named last changes fastest.
Arguments:
- pos_vel: float32 [6, 8192], P(None, ('grp', 'ja')), parts along dimension 1, may hold values from -6 to 6
- acc_jerk: float32 [6, 8192], P(None, ('grp', 'ja')), parts along dimension 1, may hold values from -6 to 6
- mass: float32 [8192], P(('grp', 'ja')), parts along dimension 0, may hold values from 7.324219e-05 to 0.0007324219
- age: float32 [8192], P(('grp', 'ja')), parts along dimension 0, may hold values from 0.125 to 0.5
- active_local: int32 [12288], P(('grp', 'ia')), parts along dimension 0, may hold values from 0 to 1023
- active_owner: int32 [12288], P(('grp', 'ia')), parts along dimension 0, may hold values from 0 to 3
Outputs:
- state: float32 [6, 12288], P(None, ('grp', 'ia')), parts along dimension 1
- forces: float32 [7, 12288], P(None, ('grp', 'ia')), parts along dimension 1
The draws below stay inside these ranges and needn't reach their ends.
There are 2 independent parts, one for each index of `grp`. The reference program is written for one: setup_inputs(seed, part) draws one part's arguments, and reference() takes and returns one part's arrays. A program takes and returns all parts, laid end to end along the dimension named above; each array names one. Nothing has to cross between parts.
All inputs are finite; a program needn't handle non-finite values.
Results may differ from the reference program's by a relative error of at most 0.0003.
Values sent between devices are 32-bit elements; how exact they have to be, the bound alone decides.
A program may use at most 64 MiB of HBM per device.

```python
import math
import jax
import jax.numpy as jnp
from jax import lax

JDEV = 1024
NSTARS = 4096
NACT = 6144
N_JA = 4


def touch_ends(result, own_key, smallest, top_value):
    longest = result.shape.index(max(result.shape))
    spots = []
    for shift in (0, 1):
        where = [jax.random.randint(jax.random.fold_in(own_key, axis), (), 0, length) for axis, length in enumerate(result.shape)]
        where[longest] = (where[longest] + shift) % result.shape[longest]
        spots.append(tuple(where))
    return result.at[spots[0]].set(smallest).at[spots[1]].set(top_value)


def level_of(own_key, dims, cuts, low, largest):
    def one(axis_at, shards_of):
        draws = jax.random.uniform(jax.random.fold_in(jax.random.fold_in(own_key, 6), axis_at), (shards_of,), jnp.float32, low / len(cuts), largest / len(cuts))
        return jnp.repeat(jnp.exp(draws), dims[axis_at] // shards_of).reshape((-1,) + (1,) * (len(dims) - axis_at - 1))

    loudness = one(*cuts[0])
    for cut in cuts[1:]:
        loudness = loudness * one(*cut)
    return loudness


def normal_values(key, dims, scale, reach, cuts=(), held_as=jnp.bfloat16):
    values = scale * jax.random.normal(key, dims, jnp.float32)
    if cuts:
        values = values * level_of(key, dims, cuts, -0.22, 0.18)
    return jnp.clip(values, -reach, reach).astype(held_as)


def setup_inputs(seed: int = 0, part: int = 0) -> dict:
    seeds = jax.random.split(jax.random.key(seed), 7)
    part_keys = jax.random.split(jax.random.fold_in(seeds[6], part), 7)
    pos_vel = normal_values(part_keys[0], (6, NSTARS), 1.0, 6.0, ((1, 4),), jnp.float32)
    acc_jerk = normal_values(part_keys[1], (6, NSTARS), 1.0, 6.0, ((1, 4),), jnp.float32)
    mass = jnp.clip(jnp.exp(math.log(0.0007324219) - 2.3025851 * jax.random.uniform(part_keys[2], (NSTARS,), jnp.float32) ** level_of(part_keys[2], (NSTARS,), ((0, 4),), -0.2, 0.2)), 7.324219041038305e-05, 0.0007324219)
    age = jnp.clip(0.125 + 0.375 * jax.random.uniform(part_keys[3], (NSTARS,), jnp.float32) ** level_of(part_keys[3], (NSTARS,), ((0, 4),), -0.2, 0.2), 0.125, 0.5)
    active_local = touch_ends(jax.random.randint(part_keys[4], (NACT,), 0, JDEV), jax.random.fold_in(part_keys[4], 1), 0, JDEV - 1).astype(jnp.int32)
    active_owner = touch_ends(jax.random.randint(part_keys[5], (NACT,), 0, N_JA), jax.random.fold_in(part_keys[5], 1), 0, N_JA - 1).astype(jnp.int32)
    return dict(pos_vel=pos_vel, acc_jerk=acc_jerk, mass=mass, age=age, active_local=active_local, active_owner=active_owner)


soften = 0.0004

def predict(pos_vel, acc_jerk, age):
    position = pos_vel[0:3]
    velocity = pos_vel[3:6]
    accel = acc_jerk[0:3]
    jolt = acc_jerk[3:6]
    step_len = age[None, :]
    new_pos = position + step_len * (velocity + step_len * (accel * 0.5 + step_len * jolt / 6.0))
    new_vel = velocity + step_len * (accel + step_len * jolt * 0.5)
    return jnp.concatenate([new_pos, new_vel], axis=0)

def pair_terms(targets, sources, masses):
    delta_pos = sources[0:3, :, None] - targets[0:3, None, :]
    delta_vel = sources[3:6, :, None] - targets[3:6, None, :]
    dist_sq = lax.optimization_barrier(jnp.sum(delta_pos * delta_pos, axis=0)) + soften
    inverse = lax.rsqrt(dist_sq)
    inv_sq = inverse * inverse
    weighted = masses[:, None] * inverse
    weighted_cube = weighted * inv_sq
    radial = 3.0 * lax.optimization_barrier(jnp.sum(delta_pos * delta_vel, axis=0)) * inv_sq
    accel = lax.optimization_barrier(jnp.sum(weighted_cube[None] * delta_pos, axis=1))
    jolt = lax.optimization_barrier(jnp.sum(weighted_cube[None] * (delta_vel - radial[None] * delta_pos), axis=1))
    potential = -lax.optimization_barrier(jnp.sum(weighted, axis=0))
    return jnp.concatenate([accel, jolt, potential[None]], axis=0)

def correct(history, forces):
    pred_pos = history[0:3]
    pred_vel = history[3:6]
    old_acc = history[6:9]
    old_jolt = history[9:12]
    step_len = history[12:13]
    new_acc = forces[0:3]
    new_jolt = forces[3:6]
    differ = old_acc - new_acc
    square = step_len * step_len
    cubed = square * step_len
    fourth = square * square
    fifth = fourth * step_len
    second = (-6.0 * differ - step_len * (4.0 * old_jolt + 2.0 * new_jolt)) / square
    third = (12.0 * differ + 6.0 * step_len * (old_jolt + new_jolt)) / cubed
    position = pred_pos + fourth / 24.0 * second + fifth / 120.0 * third
    velocity = pred_vel + cubed / 6.0 * second + fourth / 24.0 * third
    return jnp.concatenate([position, velocity], axis=0)

def reference(pos_vel, acc_jerk, mass, age, active_local, active_owner):
    predicted = predict(pos_vel, acc_jerk, age)
    chosen = (active_owner * JDEV + active_local).astype(jnp.int32)
    stacked = jnp.concatenate([predicted, acc_jerk, age[None, :]], axis=0)
    history = jnp.take(stacked, chosen, axis=1)
    targets = history[0:6]
    width = min(512, JDEV)
    nblocks = NSTARS // width
    source_blocks = predicted.reshape(6, nblocks, width).transpose(1, 0, 2)
    mass_blocks = mass.reshape(nblocks, width)

    def accumulate(total, pieces):
        return (total + pair_terms(targets, pieces[0], pieces[1]), None)
    forces, unused = lax.scan(accumulate, jnp.zeros((7, NACT), jnp.float32), (source_blocks, mass_blocks))
    state = correct(history, forces)
    return (state, forces)
```

```python
import functools
import jax
import jax.numpy as jnp
from jax import lax
from jax.experimental import pallas as pl
from jax.experimental.pallas import tpu as pltpu
from jax.sharding import PartitionSpec as P

soften = 0.0004
LANES = 128
SUB = 8
MESH = pl.DeviceIdType.MESH


def pick_columns(blocks, where_block, lane, per_block):
    total = None
    for b, tile in enumerate(blocks):
        got = jnp.take_along_axis(tile, lane, axis=1, mode="promise_in_bounds")
        total = got if total is None else jnp.where(where_block == b, got, total)
    return total


def force_kernel(
    n, chunks, unroll,
    pv, aj, mass, age, slot, owner, state_out, forces_out,
    src_all, old_all, cols, targets, results,
    src_send, src_recv, old_send, old_recv, res_send, res_recv,
):
    me = lax.axis_index("ja")
    stars = pv.shape[1]
    tiles = stars // LANES
    width = chunks * LANES

    barrier = pltpu.get_barrier_semaphore()
    for s in range(1, n):
        pl.semaphore_signal(
            barrier, inc=1, device_id={"ja": lax.rem(me + s, n)}, device_id_type=MESH
        )

    h = age[...]
    x, v = pv[0:3, :], pv[3:6, :]
    a, j = aj[0:3, :], aj[3:6, :]
    mine = src_all.at[me]
    mine[0:3, :] = x + h * (v + h * (a * 0.5 + h * j / 6.0))
    mine[3:6, :] = v + h * (a + h * j * 0.5)
    mine[6:7, :] = mass[...]
    mine[7:8, :] = h
    old_all.at[me][...] = aj[...]

    pl.semaphore_wait(barrier, n - 1)

    def exchange(ref, send, recv, s, block):
        return pltpu.make_async_remote_copy(
            src_ref=ref.at[block], dst_ref=ref.at[block],
            send_sem=send.at[s - 1], recv_sem=recv.at[s - 1],
            device_id={"ja": lax.rem(me + s, n)}, device_id_type=MESH,
        )

    order = list(range(n - 1, 0, -1))
    for s in order:
        exchange(src_all, src_send, src_recv, s, me).start()
    for s in order:
        exchange(old_all, old_send, old_recv, s, me).start()
    for s in order:
        exchange(src_all, src_send, src_recv, s, lax.rem(me + n - s, n)).wait_recv()

    def table(ref, rows):
        return [
            ref[b // tiles, 0:rows, (b % tiles) * LANES:(b % tiles + 1) * LANES]
            for b in range(n * tiles)
        ]

    for b, tile in enumerate(table(src_all, SUB)):
        cols[b * LANES:(b + 1) * LANES, :] = tile.T

    def places(c):
        start = pl.multiple_of(me * width + c * LANES, LANES)
        local = slot[:, pl.ds(start, LANES)]
        block = owner[:, pl.ds(start, LANES)] * tiles + local // LANES
        lane = local % LANES
        return (
            jnp.broadcast_to(block, (SUB, LANES)),
            jnp.broadcast_to(lane, (SUB, LANES)),
        )

    picked = []
    for c in range(chunks):
        block, lane = places(c)
        got = pick_columns(table(src_all, SUB), block, lane, tiles)
        picked.append(got)
        for row in range(6):
            targets[c, row] = jnp.broadcast_to(got[row:row + 1, :], (SUB, LANES))

    def group(g, totals):
        totals = list(totals)
        for k in range(unroll):
            start = pl.multiple_of((g * unroll + k) * SUB, SUB)
            piece = cols[pl.ds(start, SUB), :]
            qx, qy, qz, wx, wy, wz, m = [
                jnp.broadcast_to(piece[:, i:i + 1], (SUB, LANES)) for i in range(7)
            ]
            for c in range(chunks):
                rx, ry, rz = qx - targets[c, 0], qy - targets[c, 1], qz - targets[c, 2]
                ex, ey, ez = wx - targets[c, 3], wy - targets[c, 4], wz - targets[c, 5]
                d = (rx * rx + ry * ry) + (rz * rz + soften)
                z = lax.rsqrt(d)
                zz = z * z
                weight = m * z
                cube = weight * zz
                radial = ((rx * ex + ry * ey) + rz * ez) * zz
                fifth = cube * radial
                t = totals[7 * c:7 * c + 7]
                totals[7 * c:7 * c + 7] = [
                    t[0] + cube * rx, t[1] + cube * ry, t[2] + cube * rz,
                    t[3] + (cube * ex - 3.0 * (fifth * rx)),
                    t[4] + (cube * ey - 3.0 * (fifth * ry)),
                    t[5] + (cube * ez - 3.0 * (fifth * rz)),
                    t[6] + weight,
                ]
        return tuple(totals)

    zero = jnp.zeros((SUB, LANES), jnp.float32)
    totals = lax.fori_loop(0, n * stars // (SUB * unroll), group, (zero,) * (7 * chunks))

    for s in order:
        exchange(old_all, old_send, old_recv, s, lax.rem(me + n - s, n)).wait_recv()

    for c in range(chunks):
        sums = [jnp.sum(t, axis=0, keepdims=True) for t in totals[7 * c:7 * c + 7]]
        new_acc = jnp.concatenate(sums[0:3], axis=0)
        new_jolt = jnp.concatenate(sums[3:6], axis=0)
        block, lane = places(c)
        old = pick_columns(table(old_all, SUB), block, lane, tiles)
        got = picked[c]
        step = got[7:8, :]
        old_acc, old_jolt = old[0:3, :], old[3:6, :]
        differ = old_acc - new_acc
        second = -6.0 * differ - step * (4.0 * old_jolt + 2.0 * new_jolt)
        third = 12.0 * differ + 6.0 * step * (old_jolt + new_jolt)
        place = results.at[me]
        lanes = slice(c * LANES, (c + 1) * LANES)
        place[0:3, lanes] = new_acc
        place[3:6, lanes] = new_jolt
        place[6:7, lanes] = -sums[6]
        place[7:8, lanes] = step
        place[8:11, lanes] = got[0:3, :] + step * step * (second / 24.0 + third / 120.0)
        place[11:14, lanes] = got[3:6, :] + step * (second / 6.0 + third / 24.0)
        place[14:16, lanes] = jnp.zeros((2, LANES), jnp.float32)

    for s in order:
        exchange(results, res_send, res_recv, s, me).start()
    for s in order:
        exchange(results, res_send, res_recv, s, lax.rem(me + n - s, n)).wait_recv()
    for k in range(n):
        forces_out[:, k * width:(k + 1) * width] = results[k, 0:7, :]
        state_out[:, k * width:(k + 1) * width] = results[k, 8:14, :]
    for s in order:
        exchange(src_all, src_send, src_recv, s, me).wait_send()
        exchange(old_all, old_send, old_recv, s, me).wait_send()
        exchange(results, res_send, res_recv, s, me).wait_send()


def fused(n, pos_vel, acc_jerk, mass, age, active_local, active_owner):
    stars = pos_vel.shape[1]
    count = active_local.shape[0]
    chunks = count // (n * LANES)
    pairs = n * stars * chunks * LANES
    vmem = pl.BlockSpec(memory_space=pltpu.VMEM)
    old = jnp.concatenate([acc_jerk, acc_jerk[0:2]], axis=0)
    return pl.pallas_call(
        functools.partial(force_kernel, n, chunks, 2),
        out_shape=(
            jax.ShapeDtypeStruct((6, count), jnp.float32),
            jax.ShapeDtypeStruct((7, count), jnp.float32),
        ),
        in_specs=[vmem] * 6,
        out_specs=(vmem, vmem),
        scratch_shapes=[
            pltpu.VMEM((n, SUB, stars), jnp.float32),
            pltpu.VMEM((n, SUB, stars), jnp.float32),
            pltpu.VMEM((n * stars, SUB), jnp.float32),
            pltpu.VMEM((chunks, 6, SUB, LANES), jnp.float32),
            pltpu.VMEM((n, 16, chunks * LANES), jnp.float32),
        ] + [pltpu.SemaphoreType.DMA((n - 1,))] * 6,
        compiler_params=pltpu.CompilerParams(
            collective_id=0, has_side_effects=True, vmem_limit_bytes=32 * 1024 * 1024
        ),
        cost_estimate=pl.CostEstimate(flops=41 * pairs, bytes_accessed=0, transcendentals=pairs),
    )(pos_vel, old, mass[None, :], age[None, :], active_local[None, :], active_owner[None, :])


def predict(pos_vel, acc_jerk, age):
    position = pos_vel[0:3]
    velocity = pos_vel[3:6]
    accel = acc_jerk[0:3]
    jolt = acc_jerk[3:6]
    step_len = age[None, :]
    new_pos = position + step_len * (velocity + step_len * (accel * 0.5 + step_len * jolt / 6.0))
    new_vel = velocity + step_len * (accel + step_len * jolt * 0.5)
    return jnp.concatenate([new_pos, new_vel], axis=0)


def pair_terms(targets, sources, masses):
    delta_pos = sources[0:3, :, None] - targets[0:3, None, :]
    delta_vel = sources[3:6, :, None] - targets[3:6, None, :]
    dist_sq = jnp.sum(delta_pos * delta_pos, axis=0) + soften
    inverse = lax.rsqrt(dist_sq)
    inv_sq = inverse * inverse
    weighted = masses[:, None] * inverse
    weighted_cube = weighted * inv_sq
    radial = 3.0 * jnp.sum(delta_pos * delta_vel, axis=0) * inv_sq
    accel = jnp.sum(weighted_cube[None] * delta_pos, axis=1)
    jolt = jnp.sum(weighted_cube[None] * (delta_vel - radial[None] * delta_pos), axis=1)
    potential = -jnp.sum(weighted, axis=0)
    return jnp.concatenate([accel, jolt, potential[None]], axis=0)


def block_terms(targets, sources, masses):
    count = targets.shape[1]
    width = min(512, count)
    nblocks = count // width
    src_count = sources.shape[1]
    src_width = min(512, src_count)
    src_blocks = src_count // src_width
    source_pieces = sources.reshape(6, src_blocks, src_width).transpose(1, 0, 2)
    mass_pieces = masses.reshape(src_blocks, src_width)
    pieces = targets.reshape(6, nblocks, width).transpose(1, 0, 2)

    def one_block(piece):

        def accumulate(total, parts):
            return (total + pair_terms(piece, parts[0], parts[1]), None)

        total, unused = lax.scan(
            accumulate, jnp.zeros((7, width), jnp.float32), (source_pieces, mass_pieces)
        )
        return total

    results = lax.map(one_block, pieces)
    return results.transpose(1, 0, 2).reshape(7, count)


def correct(history, forces):
    pred_pos = history[0:3]
    pred_vel = history[3:6]
    old_acc = history[6:9]
    old_jolt = history[9:12]
    step_len = history[12:13]
    new_acc = forces[0:3]
    new_jolt = forces[3:6]
    differ = old_acc - new_acc
    square = step_len * step_len
    cubed = square * step_len
    fourth = square * square
    fifth = fourth * step_len
    second = (-6.0 * differ - step_len * (4.0 * old_jolt + 2.0 * new_jolt)) / square
    third = (12.0 * differ + 6.0 * step_len * (old_jolt + new_jolt)) / cubed
    position = pred_pos + fourth / 24.0 * second + fifth / 120.0 * third
    velocity = pred_vel + cubed / 6.0 * second + fourth / 24.0 * third
    return jnp.concatenate([position, velocity], axis=0)


def local(pos_vel, acc_jerk, mass, age, active_local, active_owner):
    shard_rank = lax.axis_index("ja")
    predicted = predict(pos_vel, acc_jerk, age)
    stacked = jnp.concatenate([predicted, acc_jerk, age[None, :]], axis=0)
    picked = jnp.take(stacked, active_local, axis=1)
    owned = active_owner == shard_rank
    contrib = jnp.where(owned[None, :], picked, 0.0)
    history = lax.psum(contrib, "ja")
    partial_value = block_terms(history[0:6], predicted, mass)
    forces = lax.psum(partial_value, "ja")
    state = correct(history, forces)
    return (state, forces)


def solution(mesh):
    n = mesh.shape["ja"]

    def run(*args):
        count, stars = args[4].shape[0], args[0].shape[1]
        if n > 1 and count % (n * LANES) == 0 and stars % LANES == 0:
            return fused(n, *args)
        return local(*args)

    return jax.shard_map(
        run,
        mesh=mesh,
        in_specs=(
            P(None, ("grp", "ja")),
            P(None, ("grp", "ja")),
            P(("grp", "ja")),
            P(("grp", "ja")),
            P(("grp", "ia")),
            P(("grp", "ia")),
        ),
        out_specs=(P(None, ("grp", "ia")), P(None, ("grp", "ia"))),
        check_vma=False,
    )
```

```python
import functools
import jax
import jax.numpy as jnp
from jax import lax
from jax.experimental import pallas as pl
from jax.experimental.pallas import tpu as pltpu
from jax.sharding import PartitionSpec as P

soften = 0.0004
LANES = 128
SUB = 8
MESH = pl.DeviceIdType.MESH


def pick_columns(blocks, where_block, lane):
    total = None
    for b, tile in enumerate(blocks):
        got = jnp.take_along_axis(tile, lane, axis=1, mode="promise_in_bounds")
        total = got if total is None else jnp.where(where_block == b, got, total)
    return total


def force_kernel(
    n, chunks, pair_rows,
    pv, aj, mass, age, slot, owner, state_out, forces_out,
    src_all, old_all, wide, picked, targets, sums, results,
    src_send, src_recv, old_send, old_recv, res_send, res_recv,
):
    me = lax.axis_index("ja")
    stars = pv.shape[1]
    tiles = stars // LANES
    rows = pair_rows * SUB

    barrier = pltpu.get_barrier_semaphore()
    for s in range(1, n):
        pl.semaphore_signal(
            barrier, inc=1, device_id={"ja": lax.rem(me + s, n)}, device_id_type=MESH
        )

    h = age[...]
    x, v = pv[0:3, :], pv[3:6, :]
    a, j = aj[0:3, :], aj[3:6, :]
    mine = src_all.at[me]
    mine[0:3, :] = x + h * (v + h * (a * 0.5 + h * j / 6.0))
    mine[3:6, :] = v + h * (a + h * j * 0.5)
    mine[6:7, :] = mass[...]
    mine[7:8, :] = h
    old = old_all.at[me]
    old[0:6, :] = aj[...]
    old[6:8, :] = jnp.zeros((2, stars), jnp.float32)

    pl.semaphore_wait(barrier, n - 1)

    def exchange(ref, send, recv, s, block):
        return pltpu.make_async_remote_copy(
            src_ref=ref.at[block], dst_ref=ref.at[block],
            send_sem=send.at[s - 1], recv_sem=recv.at[s - 1],
            device_id={"ja": lax.rem(me + s, n)}, device_id_type=MESH,
        )

    def exchange_result(s, block, c):
        at = c * (n - 1) + (s - 1)
        return pltpu.make_async_remote_copy(
            src_ref=results.at[block, c], dst_ref=results.at[block, c],
            send_sem=res_send.at[at], recv_sem=res_recv.at[at],
            device_id={"ja": lax.rem(me + s, n)}, device_id_type=MESH,
        )

    def widen(block):
        for b in range(tiles):
            tile = src_all[block, :, b * LANES:(b + 1) * LANES]
            for i in range(7):
                wide[block * tiles + b, i] = jnp.broadcast_to(tile[i:i + 1, :], (SUB, LANES))

    order = list(range(n - 1, 0, -1))
    for s in order:
        exchange(src_all, src_send, src_recv, s, me).start()
    for s in order:
        exchange(old_all, old_send, old_recv, s, me).start()
    widen(me)
    for s in range(1, n):
        block = lax.rem(me + n - s, n)
        exchange(src_all, src_send, src_recv, s, block).wait_recv()
        widen(block)

    def table(ref):
        return [
            ref[b // tiles, :, (b % tiles) * LANES:(b % tiles + 1) * LANES]
            for b in range(n * tiles)
        ]

    def places(c):
        at = pl.ds(me * chunks + c, 1)
        local = slot[at, :]
        block = owner[at, :] * tiles + local // LANES
        lane = local % LANES
        return (
            jnp.broadcast_to(block, (SUB, LANES)),
            jnp.broadcast_to(lane, (SUB, LANES)),
        )

    for c in range(chunks):
        block, lane = places(c)
        got = pick_columns(table(src_all), block, lane)
        picked[c] = got
        turned = got.T
        for t in range(LANES // SUB):
            for i in range(6):
                targets[c * (LANES // SUB) + t, i] = jnp.broadcast_to(
                    turned[t * SUB:(t + 1) * SUB, i:i + 1], (SUB, LANES)
                )

    def chunk(c, carry):
        def few(t, carry):
            first = (c * (LANES // rows) + t) * pair_rows
            aims = [[targets[first + k, i] for i in range(6)] for k in range(pair_rows)]

            def tile(b, totals):
                qx, qy, qz, wx, wy, wz, m = [wide[b, i] for i in range(7)]
                news = []
                for k in range(pair_rows):
                    px, py, pz, ux, uy, uz = aims[k]
                    rx, ry, rz = qx - px, qy - py, qz - pz
                    ex, ey, ez = wx - ux, wy - uy, wz - uz
                    d = (rx * rx + ry * ry) + (rz * rz + soften)
                    z = lax.rsqrt(d)
                    zz = z * z
                    weight = m * z
                    cube = weight * zz
                    radial = ((rx * ex + ry * ey) + rz * ez) * zz
                    ax, ay, az = cube * rx, cube * ry, cube * rz
                    terms = (
                        ax, ay, az, cube * ex, cube * ey, cube * ez,
                        radial * ax, radial * ay, radial * az, weight,
                    )
                    news += [p + q for p, q in zip(totals[10 * k:10 * k + 10], terms)]
                return tuple(news)

            zero = jnp.zeros((SUB, LANES), jnp.float32)
            count = n * tiles
            totals = lax.fori_loop(0, count, tile, (zero,) * (10 * pair_rows), unroll=count)
            for k in range(pair_rows):
                at = pl.ds(pl.multiple_of(t * rows + k * SUB, SUB), SUB)
                v = totals[10 * k:10 * k + 10]
                for i in range(3):
                    sums[i, at, :] = v[i]
                    sums[3 + i, at, :] = v[3 + i] - 3.0 * v[6 + i]
                sums[6, at, :] = v[9]
            return carry

        lax.fori_loop(0, LANES // rows, few, 0)

        @pl.when(c == 0)
        def _():
            for s in order:
                exchange(old_all, old_send, old_recv, s, lax.rem(me + n - s, n)).wait_recv()

        ones = jnp.ones((SUB, LANES), jnp.float32)
        total = [
            lax.dot_general(
                ones, sums[q], (((1,), (1,)), ((), ())),
                precision=lax.Precision.HIGHEST, preferred_element_type=jnp.float32,
            )[0:1, :]
            for q in range(7)
        ]
        new_acc = jnp.concatenate(total[0:3], axis=0)
        new_jolt = jnp.concatenate(total[3:6], axis=0)
        block, lane = places(c)
        old = pick_columns(table(old_all), block, lane)
        got = picked[c]
        step = got[7:8, :]
        old_acc, old_jolt = old[0:3, :], old[3:6, :]
        differ = old_acc - new_acc
        second = -6.0 * differ - step * (4.0 * old_jolt + 2.0 * new_jolt)
        third = 12.0 * differ + 6.0 * step * (old_jolt + new_jolt)
        place = results.at[me, c]
        place[0:3, :] = new_acc
        place[3:6, :] = new_jolt
        place[6:7, :] = -total[6]
        place[7:8, :] = step
        place[8:11, :] = got[0:3, :] + step * step * (second / 24.0 + third / 120.0)
        place[11:14, :] = got[3:6, :] + step * (second / 6.0 + third / 24.0)
        place[14:16, :] = jnp.zeros((2, LANES), jnp.float32)
        for s in order:
            exchange_result(s, me, c).start()
        return carry

    lax.fori_loop(0, chunks, chunk, 0)

    for c in range(chunks):
        for s in order:
            exchange_result(s, lax.rem(me + n - s, n), c).wait_recv()
    for k in range(n):
        for c in range(chunks):
            at = (k * chunks + c) * LANES
            forces_out[:, at:at + LANES] = results[k, c, 0:7, :]
            state_out[:, at:at + LANES] = results[k, c, 8:14, :]
    for s in order:
        exchange(src_all, src_send, src_recv, s, me).wait_send()
        exchange(old_all, old_send, old_recv, s, me).wait_send()
        for c in range(chunks):
            exchange_result(s, me, c).wait_send()


def fused(n, pos_vel, acc_jerk, mass, age, active_local, active_owner):
    stars = pos_vel.shape[1]
    count = active_local.shape[0]
    chunks = count // (n * LANES)
    groups = chunks * LANES // SUB
    pairs = n * stars * chunks * LANES
    vmem = pl.BlockSpec(memory_space=pltpu.VMEM)
    dma = pltpu.SemaphoreType.DMA
    return pl.pallas_call(
        functools.partial(force_kernel, n, chunks, 2),
        out_shape=(
            jax.ShapeDtypeStruct((6, count), jnp.float32),
            jax.ShapeDtypeStruct((7, count), jnp.float32),
        ),
        in_specs=[vmem] * 6,
        out_specs=(vmem, vmem),
        scratch_shapes=[
            pltpu.VMEM((n, SUB, stars), jnp.float32),
            pltpu.VMEM((n, SUB, stars), jnp.float32),
            pltpu.VMEM((n * stars // LANES, 7, SUB, LANES), jnp.float32),
            pltpu.VMEM((chunks, SUB, LANES), jnp.float32),
            pltpu.VMEM((groups, 6, SUB, LANES), jnp.float32),
            pltpu.VMEM((7, LANES, LANES), jnp.float32),
            pltpu.VMEM((n, chunks, 16, LANES), jnp.float32),
        ] + [dma((n - 1,))] * 4 + [dma(((n - 1) * chunks,))] * 2,
        compiler_params=pltpu.CompilerParams(
            collective_id=0, has_side_effects=True, vmem_limit_bytes=32 * 1024 * 1024
        ),
        cost_estimate=pl.CostEstimate(flops=41 * pairs, bytes_accessed=0, transcendentals=pairs),
    )(
        pos_vel, acc_jerk, mass[None, :], age[None, :],
        active_local.reshape(-1, LANES), active_owner.reshape(-1, LANES),
    )


def predict(pos_vel, acc_jerk, age):
    position = pos_vel[0:3]
    velocity = pos_vel[3:6]
    accel = acc_jerk[0:3]
    jolt = acc_jerk[3:6]
    step_len = age[None, :]
    new_pos = position + step_len * (velocity + step_len * (accel * 0.5 + step_len * jolt / 6.0))
    new_vel = velocity + step_len * (accel + step_len * jolt * 0.5)
    return jnp.concatenate([new_pos, new_vel], axis=0)


def pair_terms(targets, sources, masses):
    delta_pos = sources[0:3, :, None] - targets[0:3, None, :]
    delta_vel = sources[3:6, :, None] - targets[3:6, None, :]
    dist_sq = jnp.sum(delta_pos * delta_pos, axis=0) + soften
    inverse = lax.rsqrt(dist_sq)
    inv_sq = inverse * inverse
    weighted = masses[:, None] * inverse
    weighted_cube = weighted * inv_sq
    radial = 3.0 * jnp.sum(delta_pos * delta_vel, axis=0) * inv_sq
    accel = jnp.sum(weighted_cube[None] * delta_pos, axis=1)
    jolt = jnp.sum(weighted_cube[None] * (delta_vel - radial[None] * delta_pos), axis=1)
    potential = -jnp.sum(weighted, axis=0)
    return jnp.concatenate([accel, jolt, potential[None]], axis=0)


def block_terms(targets, sources, masses):
    count = targets.shape[1]
    width = min(512, count)
    nblocks = count // width
    src_count = sources.shape[1]
    src_width = min(512, src_count)
    src_blocks = src_count // src_width
    source_pieces = sources.reshape(6, src_blocks, src_width).transpose(1, 0, 2)
    mass_pieces = masses.reshape(src_blocks, src_width)
    pieces = targets.reshape(6, nblocks, width).transpose(1, 0, 2)

    def one_block(piece):

        def accumulate(total, parts):
            return (total + pair_terms(piece, parts[0], parts[1]), None)

        total, unused = lax.scan(
            accumulate, jnp.zeros((7, width), jnp.float32), (source_pieces, mass_pieces)
        )
        return total

    results = lax.map(one_block, pieces)
    return results.transpose(1, 0, 2).reshape(7, count)


def correct(history, forces):
    pred_pos = history[0:3]
    pred_vel = history[3:6]
    old_acc = history[6:9]
    old_jolt = history[9:12]
    step_len = history[12:13]
    new_acc = forces[0:3]
    new_jolt = forces[3:6]
    differ = old_acc - new_acc
    square = step_len * step_len
    cubed = square * step_len
    fourth = square * square
    fifth = fourth * step_len
    second = (-6.0 * differ - step_len * (4.0 * old_jolt + 2.0 * new_jolt)) / square
    third = (12.0 * differ + 6.0 * step_len * (old_jolt + new_jolt)) / cubed
    position = pred_pos + fourth / 24.0 * second + fifth / 120.0 * third
    velocity = pred_vel + cubed / 6.0 * second + fourth / 24.0 * third
    return jnp.concatenate([position, velocity], axis=0)


def local(pos_vel, acc_jerk, mass, age, active_local, active_owner):
    shard_rank = lax.axis_index("ja")
    predicted = predict(pos_vel, acc_jerk, age)
    stacked = jnp.concatenate([predicted, acc_jerk, age[None, :]], axis=0)
    picked = jnp.take(stacked, active_local, axis=1)
    owned = active_owner == shard_rank
    contrib = jnp.where(owned[None, :], picked, 0.0)
    history = lax.psum(contrib, "ja")
    partial_value = block_terms(history[0:6], predicted, mass)
    forces = lax.psum(partial_value, "ja")
    state = correct(history, forces)
    return (state, forces)


def solution(mesh):
    n = mesh.shape["ja"]

    def run(*args):
        count, stars = args[4].shape[0], args[0].shape[1]
        if n > 1 and count % (n * LANES) == 0 and stars % LANES == 0:
            return fused(n, *args)
        return local(*args)

    return jax.shard_map(
        run,
        mesh=mesh,
        in_specs=(
            P(None, ("grp", "ja")),
            P(None, ("grp", "ja")),
            P(("grp", "ja")),
            P(("grp", "ja")),
            P(("grp", "ia")),
            P(("grp", "ia")),
        ),
        out_specs=(P(None, ("grp", "ia")), P(None, ("grp", "ia"))),
        check_vma=False,
    )
```
